128 devices in a mesh: ent: 128 (over z, y, x, core).
Axes of the slice: x: 4, y: 4, z: 4, core: 2. Of those that a mesh axis runs over, the one named last changes fastest.
Arguments:
- mentions: bfloat16 [131072, 768], P('ent'), may hold values from -6 to 6
- table: bfloat16 [524288, 768], P('ent'), may hold values from -2 to 2
- picks: int32 [128, 8], P('ent'), may hold values from 0 to 15
- gold: int32 [131072], P('ent'), may hold values from 0 to 2047
Outputs:
- loss: float32 [], replicated
- d_mentions: float32 [131072, 768], P('ent')
- d_table: float32 [524288, 768], P('ent')
The draws below stay inside these ranges and needn't reach their ends.
All inputs are finite; a program needn't handle non-finite values.
Results may differ from the reference program's by a relative error of at most 0.002.
Values may be sent and summed in bfloat16 or wider, within the bound.
A program may use at most 128 MiB of HBM per device.

```python
import jax
import jax.numpy as jnp
from jax import lax

D = 768
ENT_DEV = 4096
BLK = 256
ROUNDS = 8
MEN = 1024
BPD = 16
CAND = 2048
ENTITIES = 524288
MENTIONS = 131072
N_ENT = 128


def shared_sign(key):
    sign_key = jax.random.fold_in(key, 7301)
    flips = jax.random.bernoulli(sign_key, 0.5, (D,))
    return jnp.where(flips, 1.0, -1.0).astype(jnp.float32)


def draw_mentions(key, part):
    base = jax.random.fold_in(key, 1101)
    k_bulk = jax.random.fold_in(base, 2)
    k_pos = jax.random.fold_in(base, 3)
    k_extra = jax.random.fold_in(base, 4)
    k_mag = jax.random.fold_in(base, 5)
    bulk = jnp.clip(jax.random.normal(k_bulk, (MENTIONS, D), jnp.float32), -5.0, 5.0)
    rows = jnp.arange(MENTIONS, dtype=jnp.int32)
    within = rows % MEN
    device = rows // MEN
    position = jax.random.randint(k_pos, (MENTIONS // MEN,), 0, MEN, dtype=jnp.int32)
    chosen = within == jnp.take(position, device)
    extra = jax.random.randint(k_extra, (MENTIONS,), 0, 16, dtype=jnp.int32) == 0
    magnitude = jnp.where(chosen, 6.0, jax.random.uniform(k_mag, (MENTIONS,), jnp.float32, 4.0, 6.0))
    planted = shared_sign(key)[None, :] * magnitude[:, None]
    aligned = jnp.logical_or(chosen, extra)
    return jnp.where(aligned[:, None], planted, bulk).astype(jnp.bfloat16)


def draw_table(key, part):
    base = jax.random.fold_in(key, 2203)
    k_level = jax.random.fold_in(base, 1)
    k_drop = jax.random.fold_in(base, 2)
    k_bulk = jax.random.fold_in(base, 4)
    nblock = ENTITIES // BLK
    rows = jnp.arange(ENTITIES, dtype=jnp.int32)
    within = rows % BLK
    block = rows // BLK
    strength = jax.random.uniform(k_level, (nblock,), jnp.float32, 45.0, 67.0)
    lowered = jax.random.uniform(k_drop, (nblock,), jnp.float32, 0.3, 0.45)
    level = jnp.take(strength, block) - jnp.where(within == 1, jnp.take(lowered, block), 0.0)
    columns = jnp.arange(D, dtype=jnp.int32)
    alternate = jnp.where(columns % 2 == 0, 0.5, -0.5).astype(jnp.float32)
    profile = jnp.where(within[:, None] == 0, 1.0 + alternate[None, :], 1.0 - alternate[None, :])
    planted = shared_sign(key)[None, :] * profile * (level / jnp.float32(D))[:, None]
    inverse_root = 1.0 / jnp.sqrt(jnp.float32(D))
    bulk = jnp.clip(jax.random.normal(k_bulk, (ENTITIES, D), jnp.float32), -4.0, 4.0) * inverse_root
    return jnp.where((within < 2)[:, None], planted, bulk).astype(jnp.bfloat16)


def with_ends(array, stream_key, least, largest):
    spot = [jax.random.randint(jax.random.fold_in(stream_key, axis), (), 0, length) for axis, length in enumerate(array.shape)]
    widest = array.shape.index(max(array.shape))
    next_to = spot[:widest] + [(spot[widest] + 1) % array.shape[widest]] + spot[widest + 1:]
    return array.at[tuple(spot)].set(least).at[tuple(next_to)].set(largest)


def setup_inputs(seed: int = 0) -> dict:
    key_list = jax.random.split(jax.random.key(seed), 5)
    mentions = draw_mentions(jax.random.fold_in(key_list[4], 71), 0)
    table = draw_table(jax.random.fold_in(key_list[4], 71), 0)
    picks = with_ends(jax.random.randint(key_list[2], (N_ENT, ROUNDS), 0, BPD), jax.random.fold_in(key_list[2], 1), 0, BPD - 1).astype(jnp.int32)
    gold = with_ends(jax.random.randint(key_list[3], (MENTIONS,), 0, CAND), jax.random.fold_in(key_list[3], 1), 0, CAND - 1).astype(jnp.int32)
    return dict(mentions=mentions, table=table, picks=picks, gold=gold)


def reference(mentions, table, picks, gold):
    stride = N_ENT // ROUNDS
    offsets = jnp.arange(ROUNDS, dtype=jnp.int32) * stride + 1
    devices = jnp.arange(N_ENT, dtype=jnp.int32)
    owners = (devices[:, None] - offsets[None, :]) % N_ENT
    chosen = picks[owners, jnp.arange(ROUNDS, dtype=jnp.int32)[None, :]]
    starts = owners * ENT_DEV + chosen * BLK
    rows_all = (starts[:, :, None] + jnp.arange(BLK, dtype=jnp.int32)[None, None, :]).reshape(N_ENT, CAND).astype(jnp.int32)
    ment = mentions.reshape(N_ENT, MEN, D)
    golds = gold.reshape(N_ENT, MEN)

    def step(carry, inputs):
        grads, total = carry
        ment_i, gold_i, rows_i = inputs
        cand = table[rows_i]
        scores = jnp.dot(ment_i, cand.T, preferred_element_type=jnp.float32)
        top = jnp.max(scores, axis=1, keepdims=True)
        lse = top[:, 0] + jnp.log(jnp.sum(jnp.exp(scores - top), axis=1))
        target = jnp.take_along_axis(scores, gold_i[:, None], axis=1)[:, 0]
        total = total + jnp.sum(lse - target)
        onehot = (jnp.arange(CAND, dtype=jnp.int32)[None, :] == gold_i[:, None]).astype(jnp.float32)
        dscore = (jnp.exp(scores - lse[:, None]) - onehot).astype(jnp.bfloat16)
        dment = jnp.dot(dscore, cand, preferred_element_type=jnp.float32)
        dcand = jnp.dot(dscore.T, ment_i, preferred_element_type=jnp.float32)
        grads = grads.at[rows_i].add(dcand)
        return (grads, total), dment

    init = (jnp.zeros((ENTITIES, D), jnp.float32), jnp.zeros((), jnp.float32))
    (grads, total), dments = lax.scan(step, init, (ment, golds, rows_all))
    loss = total / jnp.float32(MENTIONS)
    return (loss, dments.reshape(MENTIONS, D), grads)
```

```python
import functools

import jax
import jax.numpy as jnp
from jax import lax
from jax.experimental import pallas as pl
from jax.experimental.pallas import tpu as pltpu
from jax.sharding import PartitionSpec as P

BLK = 256
ROUNDS = 8
MEN = 1024
D = 768
BPD = 16
N = 128
STRIDE = N // ROUNDS
STEPS = 8
ROWS = BLK // STEPS
AHEAD = 2
WIRE = jnp.bfloat16


def ring_peers(me):
    phases = []
    for weight, length in ((32, 4), (8, 4), (2, 4), (1, 2)):
        at = lax.rem(lax.div(me, weight), length)
        base = me - at * weight
        phases.append((at, [base + lax.rem(at + by, length) * weight for by in range(1, length)]))
    return phases


def exchange(
    picks, table, mentions, gold, ret, dm, loss,
    table_v, ment_v, send, cand, scores, dscore, gsend, dm_v, lsend, lbuf,
    local_sem, dm_sem, fsend, frecv, bsend, brecv, lsend_sem, lrecv_sem,
):
    me = lax.axis_index("ent")
    load_table = pltpu.make_async_copy(table, table_v, local_sem.at[0])
    load_table.start()
    load_mentions = pltpu.make_async_copy(mentions, ment_v, local_sem.at[1])
    load_mentions.start()

    ahead = [lax.rem(me + (j * STRIDE + 1), N) for j in range(ROUNDS)]
    behind = [lax.rem(me + (N - j * STRIDE - 1), N) for j in range(ROUNDS)]
    phases = ring_peers(me)
    peers = ahead + behind + [p for _, group in phases for p in group]
    barrier = pltpu.get_barrier_semaphore()
    for peer in peers:
        pl.semaphore_signal(barrier, inc=1, device_id=(peer,), device_id_type=pl.DeviceIdType.MESH)

    load_table.wait()
    for j in range(ROUNDS):
        send[j] = table_v[picks[0, j]]
    pl.semaphore_wait(barrier, len(peers))

    def forward(c, j):
        return pltpu.make_async_remote_copy(
            src_ref=send.at[j, pl.ds(pl.multiple_of(c * ROWS, ROWS), ROWS)],
            dst_ref=cand.at[c, pl.ds(j * ROWS, ROWS)],
            send_sem=fsend.at[c, j],
            recv_sem=frecv.at[c, j],
            device_id=(ahead[j],),
            device_id_type=pl.DeviceIdType.MESH,
        )

    def backward(c, j):
        return pltpu.make_async_remote_copy(
            src_ref=gsend.at[c, pl.ds(j * ROWS, ROWS)],
            dst_ref=ret.at[j, pl.ds(pl.multiple_of(c * ROWS, ROWS), ROWS)],
            send_sem=bsend.at[c, j],
            recv_sem=brecv.at[c, j],
            device_id=(behind[j],),
            device_id_type=pl.DeviceIdType.MESH,
        )

    for c in range(AHEAD):
        for j in range(ROUNDS):
            forward(c, j).start()

    load_mentions.wait()
    gold_row = jnp.concatenate([gold[r : r + 1, :] for r in range(MEN // 128)], axis=1)
    local = lax.broadcasted_iota(jnp.int32, (BLK, MEN), 0)
    spread = (local // ROWS) * BLK + local % ROWS

    def score_step(c, carry):
        top, total, target = carry
        for j in range(ROUNDS):
            forward(c, j).wait_recv()
        for j in range(ROUNDS):
            forward(c, j).wait_send()

        @pl.when(c + AHEAD < STEPS)
        def _():
            for j in range(ROUNDS):
                forward(c + AHEAD, j).start()

        scores[c] = lax.dot_general(
            cand[c], ment_v[...], (((1,), (1,)), ((), ())), preferred_element_type=jnp.float32
        )
        here = scores[c]
        newer = jnp.maximum(top, jnp.max(here, axis=0, keepdims=True))
        total = total * jnp.exp(top - newer) + jnp.sum(jnp.exp(here - newer), axis=0, keepdims=True)
        hit = spread == gold_row - c * ROWS
        target = target + jnp.sum(jnp.where(hit, here, 0.0), axis=0, keepdims=True)
        return newer, total, target

    row = (1, MEN)
    top, total, target = lax.fori_loop(
        0,
        STEPS,
        score_step,
        (
            jnp.full(row, -jnp.inf, jnp.float32),
            jnp.zeros(row, jnp.float32),
            jnp.zeros(row, jnp.float32),
        ),
    )
    lse = top + jnp.log(total)

    def start_phase(p, value):
        at, group = phases[p]
        lsend[p] = value
        lbuf[p, at] = value
        for d, peer in enumerate(group):
            loss_copy(p, d, at, peer).start()

    def loss_copy(p, d, at, peer):
        return pltpu.make_async_remote_copy(
            src_ref=lsend.at[p],
            dst_ref=lbuf.at[p, at],
            send_sem=lsend_sem.at[p, d],
            recv_sem=lrecv_sem.at[p, d],
            device_id=(peer,),
            device_id_type=pl.DeviceIdType.MESH,
        )

    def end_phase(p):
        at, group = phases[p]
        for d, peer in enumerate(group):
            loss_copy(p, d, at, peer).wait()
        value = lbuf[p, 0]
        for d in range(1, len(group) + 1):
            value = value + lbuf[p, d]
        return value

    start_phase(0, jnp.broadcast_to(jnp.sum(lse - target, axis=1, keepdims=True), (8, 128)))

    def gradient_step(c, _):
        hit = spread == gold_row - c * ROWS
        d = (jnp.exp(scores[c] - lse) - jnp.where(hit, 1.0, 0.0)).astype(jnp.bfloat16)
        dscore[c] = d
        gsend[c] = jnp.dot(d, ment_v[...], preferred_element_type=jnp.float32).astype(WIRE)

        @pl.when(c >= AHEAD)
        def _():
            for j in range(ROUNDS):
                backward(c - AHEAD, j).wait_send()

        for j in range(ROUNDS):
            backward(c, j).start()
        return 0

    lax.fori_loop(0, STEPS, gradient_step, 0)

    tiles = MEN // BLK
    for t in range(tiles):
        part = end_phase(t)
        if t + 1 < tiles:
            start_phase(t + 1, part)
        else:
            loss[...] = part
        columns = pl.ds(t * BLK, BLK)
        d = dscore[:, :, columns].reshape(STEPS * BLK, BLK)
        dm_v[columns, :] = lax.dot_general(
            d,
            cand[...].reshape(STEPS * BLK, D),
            (((0,), (0,)), ((), ())),
            preferred_element_type=jnp.float32,
        )
        pltpu.make_async_copy(dm_v.at[columns], dm.at[columns], dm_sem.at[t]).start()

    for t in range(tiles):
        columns = pl.ds(t * BLK, BLK)
        pltpu.make_async_copy(dm_v.at[columns], dm.at[columns], dm_sem.at[t]).wait()

    def finish(c, _):
        @pl.when(c >= STEPS - AHEAD)
        def _():
            for j in range(ROUNDS):
                backward(c, j).wait_send()

        for j in range(ROUNDS):
            backward(c, j).wait_recv()
        return 0

    lax.fori_loop(0, STEPS, finish, 0)


def collect(picks, ret, dm_in, loss_in, table_out, dm_out, loss_out, sem):
    b = pl.program_id(0)
    copy = pltpu.make_async_copy(dm_in, dm_out, sem)

    @pl.when(b == 0)
    def _():
        copy.start()
        loss_out[...] = loss_in[0:1, 0:1] * (1.0 / (N * MEN))

    table_out[...] = jnp.zeros_like(table_out)
    for j in range(ROUNDS):

        @pl.when(picks[0, j] == b)
        def _(j=j):
            table_out[...] += ret[j].astype(jnp.float32)

    @pl.when(b == BPD - 1)
    def _():
        copy.wait()


def on_device(mentions, table, picks, gold):
    vmem = pl.BlockSpec(memory_space=pltpu.VMEM)
    anywhere = pl.BlockSpec(memory_space=pl.ANY)
    ret, dm, loss = pl.pallas_call(
        exchange,
        out_shape=(
            jax.ShapeDtypeStruct((ROUNDS, BLK, D), WIRE),
            jax.ShapeDtypeStruct((MEN, D), jnp.float32),
            jax.ShapeDtypeStruct((8, 128), jnp.float32),
        ),
        in_specs=[pl.BlockSpec(memory_space=pltpu.SMEM), anywhere, anywhere, vmem],
        out_specs=(anywhere, anywhere, vmem),
        scratch_shapes=[
            pltpu.VMEM((BPD, BLK, D), jnp.bfloat16),
            pltpu.VMEM((MEN, D), jnp.bfloat16),
            pltpu.VMEM((ROUNDS, BLK, D), jnp.bfloat16),
            pltpu.VMEM((STEPS, BLK, D), jnp.bfloat16),
            pltpu.VMEM((STEPS, BLK, MEN), jnp.float32),
            pltpu.VMEM((STEPS, BLK, MEN), jnp.bfloat16),
            pltpu.VMEM((STEPS, BLK, D), WIRE),
            pltpu.VMEM((MEN, D), jnp.float32),
            pltpu.VMEM((4, 8, 128), jnp.float32),
            pltpu.VMEM((4, 4, 8, 128), jnp.float32),
            pltpu.SemaphoreType.DMA((2,)),
            pltpu.SemaphoreType.DMA((4,)),
            pltpu.SemaphoreType.DMA((STEPS, ROUNDS)),
            pltpu.SemaphoreType.DMA((STEPS, ROUNDS)),
            pltpu.SemaphoreType.DMA((STEPS, ROUNDS)),
            pltpu.SemaphoreType.DMA((STEPS, ROUNDS)),
            pltpu.SemaphoreType.DMA((4, 3)),
            pltpu.SemaphoreType.DMA((4, 3)),
        ],
        compiler_params=pltpu.CompilerParams(
            collective_id=0, has_side_effects=True, vmem_limit_bytes=56 * 2**20
        ),
        name="exchange",
    )(picks, table.reshape(BPD, BLK, D), mentions, gold.reshape(8, 128))
    d_table, d_mentions, total = pl.pallas_call(
        collect,
        grid=(BPD,),
        out_shape=(
            jax.ShapeDtypeStruct((BPD * BLK, D), jnp.float32),
            jax.ShapeDtypeStruct((MEN, D), jnp.float32),
            jax.ShapeDtypeStruct((1, 1), jnp.float32),
        ),
        in_specs=[
            pl.BlockSpec(memory_space=pltpu.SMEM),
            pl.BlockSpec((ROUNDS, BLK, D), lambda b: (0, 0, 0)),
            anywhere,
            pl.BlockSpec((8, 128), lambda b: (0, 0)),
        ],
        out_specs=(
            pl.BlockSpec((BLK, D), lambda b: (b, 0)),
            anywhere,
            pl.BlockSpec((1, 1), lambda b: (0, 0)),
        ),
        scratch_shapes=[pltpu.SemaphoreType.DMA],
        compiler_params=pltpu.CompilerParams(vmem_limit_bytes=32 * 2**20),
        name="collect",
    )(picks, ret, dm, loss)
    return total.reshape(()), d_mentions, d_table


def solution(mesh):
    return jax.shard_map(
        on_device,
        mesh=mesh,
        in_specs=(P("ent", None), P("ent", None), P("ent", None), P("ent")),
        out_specs=(P(), P("ent", None), P("ent", None)),
        check_vma=False,
    )
```

```python
import functools

import jax
import jax.numpy as jnp
from jax import lax
from jax.experimental import pallas as pl
from jax.experimental.pallas import tpu as pltpu
from jax.sharding import PartitionSpec as P

BLK = 256
ROUNDS = 8
MEN = 1024
D = 768
BPD = 16
N = 128
STRIDE = N // ROUNDS
STEPS = 8
ROWS = BLK // STEPS
AHEAD = 4
WIRE = jnp.bfloat16


def ring_peers(me):
    phases = []
    for weight, length in ((32, 4), (8, 4), (2, 4), (1, 2)):
        at = lax.rem(lax.div(me, weight), length)
        base = me - at * weight
        phases.append((at, [base + lax.rem(at + by, length) * weight for by in range(1, length)]))
    return phases


def exchange(
    picks, table, mentions, gold, ret, dm, loss,
    table_v, ment_v, send, cand, scores, dscore, gsend, lsend, lbuf,
    local_sem, fsend, frecv, bsend, brecv, lsend_sem, lrecv_sem,
):
    me = lax.axis_index("ent")
    load_table = pltpu.make_async_copy(table, table_v, local_sem.at[0])
    load_table.start()
    load_mentions = pltpu.make_async_copy(mentions, ment_v, local_sem.at[1])
    load_mentions.start()

    ahead = [lax.rem(me + (j * STRIDE + 1), N) for j in range(ROUNDS)]
    behind = [lax.rem(me + (N - j * STRIDE - 1), N) for j in range(ROUNDS)]
    phases = ring_peers(me)
    peers = ahead + behind + [p for _, group in phases for p in group]
    barrier = pltpu.get_barrier_semaphore()
    for peer in peers:
        pl.semaphore_signal(barrier, inc=1, device_id=(peer,), device_id_type=pl.DeviceIdType.MESH)

    load_table.wait()
    for j in range(ROUNDS):
        send[j] = table_v[picks[0, j]]
    pl.semaphore_wait(barrier, len(peers))

    def forward(c, j):
        return pltpu.make_async_remote_copy(
            src_ref=send.at[j, pl.ds(pl.multiple_of(c * ROWS, ROWS), ROWS)],
            dst_ref=cand.at[c, pl.ds(j * ROWS, ROWS)],
            send_sem=fsend.at[c, j],
            recv_sem=frecv.at[c, j],
            device_id=(ahead[j],),
            device_id_type=pl.DeviceIdType.MESH,
        )

    def backward(c, j):
        return pltpu.make_async_remote_copy(
            src_ref=gsend.at[c, pl.ds(j * ROWS, ROWS)],
            dst_ref=ret.at[j, pl.ds(pl.multiple_of(c * ROWS, ROWS), ROWS)],
            send_sem=bsend.at[c, j],
            recv_sem=brecv.at[c, j],
            device_id=(behind[j],),
            device_id_type=pl.DeviceIdType.MESH,
        )

    for c in range(AHEAD):
        for j in range(ROUNDS):
            forward(c, j).start()

    load_mentions.wait()
    gold_row = jnp.concatenate([gold[r : r + 1, :] for r in range(MEN // 128)], axis=1)
    local = lax.broadcasted_iota(jnp.int32, (BLK, MEN), 0)
    spread = (local // ROWS) * BLK + local % ROWS

    def score_step(c, carry):
        top, total, target = carry
        for j in range(ROUNDS):
            forward(c, j).wait_recv()
        for j in range(ROUNDS):
            forward(c, j).wait_send()

        @pl.when(c + AHEAD < STEPS)
        def _():
            for j in range(ROUNDS):
                forward(c + AHEAD, j).start()

        scores[c] = lax.dot_general(
            cand[c], ment_v[...], (((1,), (1,)), ((), ())), preferred_element_type=jnp.float32
        )
        here = scores[c]
        newer = jnp.maximum(top, jnp.max(here, axis=0, keepdims=True))
        total = total * jnp.exp(top - newer) + jnp.sum(jnp.exp(here - newer), axis=0, keepdims=True)
        hit = spread == gold_row - c * ROWS
        target = target + jnp.sum(jnp.where(hit, here, 0.0), axis=0, keepdims=True)
        return newer, total, target

    row = (1, MEN)
    top, total, target = lax.fori_loop(
        0,
        STEPS,
        score_step,
        (
            jnp.full(row, -jnp.inf, jnp.float32),
            jnp.zeros(row, jnp.float32),
            jnp.zeros(row, jnp.float32),
        ),
    )
    lse = top + jnp.log(total)

    def start_phase(p, value):
        at, group = phases[p]
        lsend[p] = value
        lbuf[p, at] = value
        for d, peer in enumerate(group):
            loss_copy(p, d, at, peer).start()

    def loss_copy(p, d, at, peer):
        return pltpu.make_async_remote_copy(
            src_ref=lsend.at[p],
            dst_ref=lbuf.at[p, at],
            send_sem=lsend_sem.at[p, d],
            recv_sem=lrecv_sem.at[p, d],
            device_id=(peer,),
            device_id_type=pl.DeviceIdType.MESH,
        )

    def end_phase(p):
        at, group = phases[p]
        for d, peer in enumerate(group):
            loss_copy(p, d, at, peer).wait()
        value = lbuf[p, 0]
        for d in range(1, len(group) + 1):
            value = value + lbuf[p, d]
        return value

    start_phase(0, jnp.broadcast_to(jnp.sum(lse - target, axis=1, keepdims=True), (8, 128)))

    def gradient_step(c, _):
        hit = spread == gold_row - c * ROWS
        d = (jnp.exp(scores[c] - lse) - jnp.where(hit, 1.0, 0.0)).astype(jnp.bfloat16)
        dscore[c] = d
        gsend[c] = jnp.dot(d, ment_v[...], preferred_element_type=jnp.float32).astype(WIRE)

        @pl.when(c >= AHEAD)
        def _():
            for j in range(ROUNDS):
                backward(c - AHEAD, j).wait_send()

        for j in range(ROUNDS):
            backward(c, j).start()
        return 0

    lax.fori_loop(0, STEPS, gradient_step, 0)

    tiles = MEN // BLK
    for t in range(tiles):
        part = end_phase(t)
        if t + 1 < tiles:
            start_phase(t + 1, part)
        else:
            loss[...] = part
        columns = pl.ds(t * BLK, BLK)
        d = dscore[:, :, columns].reshape(STEPS * BLK, BLK)
        dm[columns, :] = lax.dot_general(
            d,
            cand[...].reshape(STEPS * BLK, D),
            (((0,), (0,)), ((), ())),
            preferred_element_type=jnp.float32,
        )

    def finish(c, _):
        @pl.when(c >= STEPS - AHEAD)
        def _():
            for j in range(ROUNDS):
                backward(c, j).wait_send()

        for j in range(ROUNDS):
            backward(c, j).wait_recv()
        return 0

    lax.fori_loop(0, STEPS, finish, 0)


def collect(picks, ret, dm_in, loss_in, table_out, dm_out, loss_out, zero, acc, dm_sem, zero_sem, acc_sem):
    dm_copy = pltpu.make_async_copy(dm_in, dm_out, dm_sem)
    dm_copy.start()
    zero[...] = jnp.zeros_like(zero)
    picked = [picks[0, j] for j in range(ROUNDS)]

    def clear(b):
        return pltpu.make_async_copy(zero, table_out.at[b], zero_sem.at[b])

    def store(j):
        return pltpu.make_async_copy(acc.at[j], table_out.at[picked[j]], acc_sem.at[j])

    def unused(b):
        return functools.reduce(jnp.logical_and, [p != b for p in picked])

    def first(j):
        return functools.reduce(jnp.logical_and, [picked[i] != picked[j] for i in range(j)], True)

    for b in range(BPD):

        @pl.when(unused(b))
        def _(b=b):
            clear(b).start()

    for j in range(ROUNDS):

        @pl.when(first(j))
        def _(j=j):
            acc[j] = ret[j].astype(jnp.float32)
            for i in range(j + 1, ROUNDS):

                @pl.when(picked[i] == picked[j])
                def _(i=i):
                    acc[j] += ret[i].astype(jnp.float32)

            store(j).start()

    loss_out[...] = loss_in[0:1, 0:1] * (1.0 / (N * MEN))
    for b in range(BPD):

        @pl.when(unused(b))
        def _(b=b):
            clear(b).wait()

    for j in range(ROUNDS):

        @pl.when(first(j))
        def _(j=j):
            store(j).wait()

    dm_copy.wait()


def on_device(mentions, table, picks, gold):
    vmem = pl.BlockSpec(memory_space=pltpu.VMEM)
    anywhere = pl.BlockSpec(memory_space=pl.ANY)
    ret, dm, loss = pl.pallas_call(
        exchange,
        out_shape=(
            pltpu.VMEM((ROUNDS, BLK, D), WIRE),
            pltpu.VMEM((MEN, D), jnp.float32),
            pltpu.VMEM((8, 128), jnp.float32),
        ),
        in_specs=[pl.BlockSpec(memory_space=pltpu.SMEM), anywhere, anywhere, vmem],
        out_specs=(vmem, vmem, vmem),
        scratch_shapes=[
            pltpu.VMEM((BPD, BLK, D), jnp.bfloat16),
            pltpu.VMEM((MEN, D), jnp.bfloat16),
            pltpu.VMEM((ROUNDS, BLK, D), jnp.bfloat16),
            pltpu.VMEM((STEPS, BLK, D), jnp.bfloat16),
            pltpu.VMEM((STEPS, BLK, MEN), jnp.float32),
            pltpu.VMEM((STEPS, BLK, MEN), jnp.bfloat16),
            pltpu.VMEM((STEPS, BLK, D), WIRE),
            pltpu.VMEM((4, 8, 128), jnp.float32),
            pltpu.VMEM((4, 4, 8, 128), jnp.float32),
            pltpu.SemaphoreType.DMA((2,)),
            pltpu.SemaphoreType.DMA((STEPS, ROUNDS)),
            pltpu.SemaphoreType.DMA((STEPS, ROUNDS)),
            pltpu.SemaphoreType.DMA((STEPS, ROUNDS)),
            pltpu.SemaphoreType.DMA((STEPS, ROUNDS)),
            pltpu.SemaphoreType.DMA((4, 3)),
            pltpu.SemaphoreType.DMA((4, 3)),
        ],
        compiler_params=pltpu.CompilerParams(
            collective_id=0, has_side_effects=True, vmem_limit_bytes=56 * 2**20
        ),
        name="exchange",
    )(picks, table.reshape(BPD, BLK, D), mentions, gold.reshape(8, 128))
    d_table, d_mentions, total = pl.pallas_call(
        collect,
        out_shape=(
            jax.ShapeDtypeStruct((BPD, BLK, D), jnp.float32),
            jax.ShapeDtypeStruct((MEN, D), jnp.float32),
            jax.ShapeDtypeStruct((1, 1), jnp.float32),
        ),
        in_specs=[pl.BlockSpec(memory_space=pltpu.SMEM), vmem, vmem, vmem],
        out_specs=(anywhere, anywhere, vmem),
        scratch_shapes=[
            pltpu.VMEM((BLK, D), jnp.float32),
            pltpu.VMEM((ROUNDS, BLK, D), jnp.float32),
            pltpu.SemaphoreType.DMA,
            pltpu.SemaphoreType.DMA((BPD,)),
            pltpu.SemaphoreType.DMA((ROUNDS,)),
        ],
        compiler_params=pltpu.CompilerParams(vmem_limit_bytes=24 * 2**20),
        name="collect",
    )(picks, ret, dm, loss)
    return total.reshape(()), d_mentions, d_table.reshape(BPD * BLK, D)


def solution(mesh):
    return jax.shard_map(
        on_device,
        mesh=mesh,
        in_specs=(P("ent", None), P("ent", None), P("ent", None), P("ent")),
        out_specs=(P(), P("ent", None), P("ent", None)),
        check_vma=False,
    )
```

```python
import functools

import jax
import jax.numpy as jnp
from jax import lax
from jax.experimental import pallas as pl
from jax.experimental.pallas import tpu as pltpu
from jax.sharding import PartitionSpec as P

BLK = 256
ROUNDS = 8
MEN = 1024
D = 768
BPD = 16
N = 128
STRIDE = N // ROUNDS
STEPS = 8
ROWS = BLK // STEPS
AHEAD = 4
WINDOW = 8
WIRE = jnp.bfloat16


def ring_peers(me):
    phases = []
    for weight, length in ((32, 4), (8, 4), (2, 4), (1, 2)):
        at = lax.rem(lax.div(me, weight), length)
        base = me - at * weight
        phases.append((at, [base + lax.rem(at + by, length) * weight for by in range(1, length)]))
    return phases


def exchange(
    picks, table, mentions, gold, ret, dm, loss,
    part_a, part_b, part_c, part_d, ment_v, gold_v, send, cand, scores, dscore, gsend, lsend, lbuf,
    local_sem, fsend, frecv, bsend, brecv, lsend_sem, lrecv_sem,
):
    me = lax.axis_index("ent")
    parts = (part_a, part_b, part_c, part_d)
    depth = BLK // len(parts)
    loads = [
        pltpu.make_async_copy(table.at[:, pl.ds(q * depth, depth)], part, local_sem.at[q])
        for q, part in enumerate(parts)
    ]
    load_mentions = pltpu.make_async_copy(mentions, ment_v, local_sem.at[len(parts)])
    load_gold = pltpu.make_async_copy(gold, gold_v, local_sem.at[len(parts) + 1])
    for load in loads:
        load.start()

    ahead = [lax.rem(me + (j * STRIDE + 1), N) for j in range(ROUNDS)]
    behind = [lax.rem(me + (N - j * STRIDE - 1), N) for j in range(ROUNDS)]
    phases = ring_peers(me)
    peers = ahead + behind + [p for _, group in phases for p in group]
    barrier = pltpu.get_barrier_semaphore()
    for peer in peers:
        pl.semaphore_signal(barrier, inc=1, device_id=(peer,), device_id_type=pl.DeviceIdType.MESH)
    load_mentions.start()
    load_gold.start()

    def remote(src, dst, send_sem, recv_sem, device):
        return pltpu.make_async_remote_copy(
            src_ref=src,
            dst_ref=dst,
            send_sem=send_sem,
            recv_sem=recv_sem,
            device_id=(device,),
            device_id_type=pl.DeviceIdType.MESH,
        )

    def wait_for(ref, sem):
        pltpu.make_async_copy(ref, ref, sem).wait()

    def start_forward(c):
        for j in range(ROUNDS):
            remote(
                send.at[c, pl.ds(j * ROWS, ROWS)],
                cand.at[c, pl.ds(j * ROWS, ROWS)],
                fsend.at[c],
                frecv.at[c],
                ahead[j],
            ).start()

    def start_backward(c):
        for j in range(ROUNDS):
            remote(
                gsend.at[c, pl.ds(j * ROWS, ROWS)],
                ret.at[j, pl.ds(pl.multiple_of(c * ROWS, ROWS), ROWS)],
                bsend.at[c],
                brecv.at[0],
                behind[j],
            ).start()

    for q, part in enumerate(parts):
        loads[q].wait()
        for j in range(ROUNDS):
            block = part[picks[0, j]]
            for h in range(depth // ROWS):
                send[q * (depth // ROWS) + h, j * ROWS : (j + 1) * ROWS] = block[h * ROWS : (h + 1) * ROWS]
        if q == 0:
            pl.semaphore_wait(barrier, len(peers))
        for c in range(q * (depth // ROWS), (q + 1) * (depth // ROWS)):
            if c < AHEAD:
                start_forward(c)

    load_mentions.wait()
    load_gold.wait()
    gold_row = jnp.concatenate([gold_v[r : r + 1, :] for r in range(MEN // 128)], axis=1)
    local = lax.broadcasted_iota(jnp.int32, (BLK, MEN), 0)
    spread = (local // ROWS) * BLK + local % ROWS

    def score_step(c, carry):
        top, total, target = carry
        wait_for(cand.at[c], frecv.at[c])
        wait_for(send.at[c], fsend.at[c])

        @pl.when(c + AHEAD < STEPS)
        def _():
            start_forward(c + AHEAD)

        scores[c] = lax.dot_general(
            cand[c], ment_v[...], (((1,), (1,)), ((), ())), preferred_element_type=jnp.float32
        )
        here = scores[c]
        newer = jnp.maximum(top, jnp.max(here, axis=0, keepdims=True))
        total = total * jnp.exp(top - newer) + jnp.sum(jnp.exp(here - newer), axis=0, keepdims=True)
        hit = spread == gold_row - c * ROWS
        target = target + jnp.sum(jnp.where(hit, here, 0.0), axis=0, keepdims=True)
        return newer, total, target

    row = (1, MEN)
    top, total, target = lax.fori_loop(
        0,
        STEPS,
        score_step,
        (
            jnp.full(row, -jnp.inf, jnp.float32),
            jnp.zeros(row, jnp.float32),
            jnp.zeros(row, jnp.float32),
        ),
    )
    lse = top + jnp.log(total)

    def gradient_step(c, _):
        hit = spread == gold_row - c * ROWS
        d = (jnp.exp(scores[c] - lse) - jnp.where(hit, 1.0, 0.0)).astype(jnp.bfloat16)
        dscore[c] = d
        gsend[c] = jnp.dot(d, ment_v[...], preferred_element_type=jnp.float32).astype(WIRE)

        @pl.when(c >= WINDOW)
        def _():
            wait_for(gsend.at[c - WINDOW], bsend.at[c - WINDOW])

        start_backward(c)
        return 0

    lax.fori_loop(0, STEPS, gradient_step, 0)

    def start_phase(p, value):
        at, group = phases[p]
        lsend[p] = value
        lbuf[p, at] = value
        for peer in group:
            remote(lsend.at[p], lbuf.at[p, at], lsend_sem.at[p], lrecv_sem.at[p], peer).start()

    def end_phase(p):
        count = len(phases[p][1])
        wait_for(lbuf.at[p, pl.ds(0, count)], lsend_sem.at[p])
        wait_for(lbuf.at[p, pl.ds(0, count)], lrecv_sem.at[p])
        value = lbuf[p, 0]
        for d in range(1, count + 1):
            value = value + lbuf[p, d]
        return value

    start_phase(0, jnp.broadcast_to(jnp.sum(lse - target, axis=1, keepdims=True), (8, 128)))
    tiles = MEN // BLK
    for t in range(tiles):
        columns = pl.ds(t * BLK, BLK)
        dm[columns, :] = lax.dot_general(
            dscore[:, :, columns].reshape(STEPS * BLK, BLK),
            cand[...].reshape(STEPS * BLK, D),
            (((0,), (0,)), ((), ())),
            preferred_element_type=jnp.float32,
        )
        part = end_phase(t)
        if t + 1 < tiles:
            start_phase(t + 1, part)
        else:
            loss[...] = part

    for c in range(STEPS - WINDOW, STEPS):
        wait_for(gsend.at[c], bsend.at[c])
    wait_for(ret, brecv.at[0])


def collect(picks, ret, dm_in, loss_in, table_out, dm_out, loss_out, zero, acc, dm_sem, zero_sem, acc_sem):
    dm_copy = pltpu.make_async_copy(dm_in, dm_out, dm_sem)
    dm_copy.start()
    zero[...] = jnp.zeros_like(zero)
    picked = [picks[0, j] for j in range(ROUNDS)]

    def clear(b):
        return pltpu.make_async_copy(zero, table_out.at[b], zero_sem.at[b])

    def store(j):
        return pltpu.make_async_copy(acc.at[j], table_out.at[picked[j]], acc_sem.at[j])

    def unused(b):
        return functools.reduce(jnp.logical_and, [p != b for p in picked])

    def first(j):
        return functools.reduce(jnp.logical_and, [picked[i] != picked[j] for i in range(j)], True)

    for b in range(BPD):

        @pl.when(unused(b))
        def _(b=b):
            clear(b).start()

    for j in range(ROUNDS):

        @pl.when(first(j))
        def _(j=j):
            acc[j] = ret[j].astype(jnp.float32)
            for i in range(j + 1, ROUNDS):

                @pl.when(picked[i] == picked[j])
                def _(i=i):
                    acc[j] += ret[i].astype(jnp.float32)

            store(j).start()

    loss_out[...] = loss_in[0:1, 0:1] * (1.0 / (N * MEN))
    for b in range(BPD):

        @pl.when(unused(b))
        def _(b=b):
            clear(b).wait()

    for j in range(ROUNDS):

        @pl.when(first(j))
        def _(j=j):
            store(j).wait()

    dm_copy.wait()


def on_device(mentions, table, picks, gold):
    vmem = pl.BlockSpec(memory_space=pltpu.VMEM)
    anywhere = pl.BlockSpec(memory_space=pl.ANY)
    ret, dm, loss = pl.pallas_call(
        exchange,
        out_shape=(
            pltpu.VMEM((ROUNDS, BLK, D), WIRE),
            pltpu.VMEM((MEN, D), jnp.float32),
            pltpu.VMEM((8, 128), jnp.float32),
        ),
        in_specs=[pl.BlockSpec(memory_space=pltpu.SMEM), anywhere, anywhere, anywhere],
        out_specs=(vmem, vmem, vmem),
        scratch_shapes=[
            *(pltpu.VMEM((BPD, BLK // 4, D), jnp.bfloat16) for _ in range(4)),
            pltpu.VMEM((MEN, D), jnp.bfloat16),
            pltpu.VMEM((8, 128), jnp.int32),
            pltpu.VMEM((STEPS, BLK, D), jnp.bfloat16),
            pltpu.VMEM((STEPS, BLK, D), jnp.bfloat16),
            pltpu.VMEM((STEPS, BLK, MEN), jnp.float32),
            pltpu.VMEM((STEPS, BLK, MEN), jnp.bfloat16),
            pltpu.VMEM((STEPS, BLK, D), WIRE),
            pltpu.VMEM((4, 8, 128), jnp.float32),
            pltpu.VMEM((4, 4, 8, 128), jnp.float32),
            pltpu.SemaphoreType.DMA((6,)),
            pltpu.SemaphoreType.DMA((STEPS,)),
            pltpu.SemaphoreType.DMA((STEPS,)),
            pltpu.SemaphoreType.DMA((STEPS,)),
            pltpu.SemaphoreType.DMA((1,)),
            pltpu.SemaphoreType.DMA((4,)),
            pltpu.SemaphoreType.DMA((4,)),
        ],
        compiler_params=pltpu.CompilerParams(
            collective_id=0, has_side_effects=True, vmem_limit_bytes=56 * 2**20
        ),
        name="exchange",
    )(picks, table.reshape(BPD, BLK, D), mentions, gold.reshape(8, 128))
    d_table, d_mentions, total = pl.pallas_call(
        collect,
        out_shape=(
            jax.ShapeDtypeStruct((BPD, BLK, D), jnp.float32),
            jax.ShapeDtypeStruct((MEN, D), jnp.float32),
            jax.ShapeDtypeStruct((1, 1), jnp.float32),
        ),
        in_specs=[pl.BlockSpec(memory_space=pltpu.SMEM), vmem, vmem, vmem],
        out_specs=(anywhere, anywhere, vmem),
        scratch_shapes=[
            pltpu.VMEM((BLK, D), jnp.float32),
            pltpu.VMEM((ROUNDS, BLK, D), jnp.float32),
            pltpu.SemaphoreType.DMA,
            pltpu.SemaphoreType.DMA((BPD,)),
            pltpu.SemaphoreType.DMA((ROUNDS,)),
        ],
        compiler_params=pltpu.CompilerParams(vmem_limit_bytes=24 * 2**20),
        name="collect",
    )(picks, ret, dm, loss)
    return total.reshape(()), d_mentions, d_table.reshape(BPD * BLK, D)


def solution(mesh):
    return jax.shard_map(
        on_device,
        mesh=mesh,
        in_specs=(P("ent", None), P("ent", None), P("ent", None), P("ent")),
        out_specs=(P(), P("ent", None), P("ent", None)),
        check_vma=False,
    )
```

```python
import functools

import jax
import jax.numpy as jnp
from jax import lax
from jax.experimental import pallas as pl
from jax.experimental.pallas import tpu as pltpu
from jax.sharding import PartitionSpec as P

BLK = 256
ROUNDS = 8
MEN = 1024
D = 768
BPD = 16
N = 128
STRIDE = N // ROUNDS
STEPS = 8
ROWS = BLK // STEPS
AHEAD = 4
WIRE = jnp.bfloat16


def ring_peers(me):
    phases = []
    for weight, length in ((32, 4), (8, 4), (2, 4), (1, 2)):
        at = lax.rem(lax.div(me, weight), length)
        base = me - at * weight
        phases.append((at, [base + lax.rem(at + by, length) * weight for by in range(1, length)]))
    return phases


def exchange(
    picks, table, mentions, gold, ret, dm, loss,
    part_a, part_b, part_c, part_d, ment_v, gold_v, send, cand, scores, dscore, gsend, lsend, lbuf,
    local_sem, fsend, frecv, bsend, brecv, lsend_sem, lrecv_sem,
):
    me = lax.axis_index("ent")
    parts = (part_a, part_b, part_c, part_d)
    depth = BLK // len(parts)
    loads = [
        pltpu.make_async_copy(table.at[:, pl.ds(q * depth, depth)], part, local_sem.at[q])
        for q, part in enumerate(parts)
    ]
    load_mentions = pltpu.make_async_copy(mentions, ment_v, local_sem.at[len(parts)])
    load_gold = pltpu.make_async_copy(gold, gold_v, local_sem.at[len(parts) + 1])
    for load in loads:
        load.start()

    ahead = [lax.rem(me + (j * STRIDE + 1), N) for j in range(ROUNDS)]
    behind = [lax.rem(me + (N - j * STRIDE - 1), N) for j in range(ROUNDS)]
    phases = ring_peers(me)
    peers = ahead + behind + [p for _, group in phases for p in group]
    barrier = pltpu.get_barrier_semaphore()
    for peer in peers:
        pl.semaphore_signal(barrier, inc=1, device_id=(peer,), device_id_type=pl.DeviceIdType.MESH)
    load_mentions.start()
    load_gold.start()

    def remote(src, dst, send_sem, recv_sem, device):
        return pltpu.make_async_remote_copy(
            src_ref=src,
            dst_ref=dst,
            send_sem=send_sem,
            recv_sem=recv_sem,
            device_id=(device,),
            device_id_type=pl.DeviceIdType.MESH,
        )

    def wait_for(ref, sem):
        pltpu.make_async_copy(ref, ref, sem).wait()

    def start_forward(c):
        for j in range(ROUNDS):
            remote(
                send.at[c, pl.ds(j * ROWS, ROWS)],
                cand.at[c, pl.ds(j * ROWS, ROWS)],
                fsend.at[c],
                frecv.at[c],
                ahead[j],
            ).start()

    def start_backward(c, which):
        for j in which:
            remote(
                gsend.at[c, pl.ds(j * ROWS, ROWS)],
                ret.at[j, pl.ds(pl.multiple_of(c * ROWS, ROWS), ROWS)],
                bsend.at[0],
                brecv.at[0],
                behind[j],
            ).start()

    for q, part in enumerate(parts):
        loads[q].wait()
        for j in range(ROUNDS):
            block = part[picks[0, j]]
            for h in range(depth // ROWS):
                send[q * (depth // ROWS) + h, j * ROWS : (j + 1) * ROWS] = block[h * ROWS : (h + 1) * ROWS]
        if q == 0:
            pl.semaphore_wait(barrier, len(peers))
        for c in range(q * (depth // ROWS), (q + 1) * (depth // ROWS)):
            if c < AHEAD:
                start_forward(c)

    load_mentions.wait()
    load_gold.wait()
    gold_row = jnp.concatenate([gold_v[r : r + 1, :] for r in range(MEN // 128)], axis=1)
    local = lax.broadcasted_iota(jnp.int32, (BLK, MEN), 0)
    spread = (local // ROWS) * BLK + local % ROWS

    def score_step(c, carry):
        top, total = carry
        wait_for(cand.at[c], frecv.at[c])

        @pl.when(c + AHEAD < STEPS)
        def _():
            wait_for(send.at[c], fsend.at[c])
            start_forward(c + AHEAD)

        scores[c] = lax.dot_general(
            cand[c], ment_v[...], (((1,), (1,)), ((), ())), preferred_element_type=jnp.float32
        )
        here = scores[c]
        newer = jnp.maximum(top, jnp.max(here, axis=0, keepdims=True))
        total = total * jnp.exp(top - newer) + jnp.sum(jnp.exp(here - newer), axis=0, keepdims=True)
        return newer, total

    row = (1, MEN)
    top, total = lax.fori_loop(
        0,
        STEPS,
        score_step,
        (
            jnp.full(row, -jnp.inf, jnp.float32),
            jnp.zeros(row, jnp.float32),
        ),
    )
    lse = top + jnp.log(total)

    def gradient_step(c, target):
        half = BLK // 2
        hit = spread == gold_row - c * ROWS
        for h in range(2):
            rows = slice(h * half, (h + 1) * half)
            d = (jnp.exp(scores[c, rows] - lse) - jnp.where(hit[rows], 1.0, 0.0)).astype(jnp.bfloat16)
            dscore[c, rows] = d
            gsend[c, rows] = jnp.dot(d, ment_v[...], preferred_element_type=jnp.float32).astype(WIRE)
            start_backward(c, range(h * ROUNDS // 2, (h + 1) * ROUNDS // 2))
        return target + jnp.sum(jnp.where(hit, scores[c], 0.0), axis=0, keepdims=True)

    target = lax.fori_loop(0, STEPS, gradient_step, jnp.zeros(row, jnp.float32))

    def start_phase(p, value):
        at, group = phases[p]
        lsend[p] = value
        lbuf[p, at] = value
        for peer in group:
            remote(lsend.at[p], lbuf.at[p, at], lsend_sem.at[p], lrecv_sem.at[p], peer).start()

    def end_phase(p):
        count = len(phases[p][1])
        wait_for(lbuf.at[p, pl.ds(0, count)], lsend_sem.at[p])
        wait_for(lbuf.at[p, pl.ds(0, count)], lrecv_sem.at[p])
        value = lbuf[p, 0]
        for d in range(1, count + 1):
            value = value + lbuf[p, d]
        return value

    start_phase(0, jnp.broadcast_to(jnp.sum(lse - target, axis=1, keepdims=True), (8, 128)))
    tiles = MEN // BLK
    for t in range(tiles):
        columns = pl.ds(t * BLK, BLK)
        dm[columns, :] = lax.dot_general(
            dscore[:, :, columns].reshape(STEPS * BLK, BLK),
            cand[...].reshape(STEPS * BLK, D),
            (((0,), (0,)), ((), ())),
            preferred_element_type=jnp.float32,
        )
        part = end_phase(t)
        if t + 1 < tiles:
            start_phase(t + 1, part)
        else:
            loss[...] = part

    for c in range(STEPS - AHEAD, STEPS):
        wait_for(send.at[c], fsend.at[c])
    wait_for(gsend, bsend.at[0])
    wait_for(ret, brecv.at[0])


def collect(picks, ret, dm_in, loss_in, table_out, dm_out, loss_out, zero, acc, dm_sem, zero_sem, acc_sem):
    dm_copy = pltpu.make_async_copy(dm_in, dm_out, dm_sem)
    dm_copy.start()
    zero[...] = jnp.zeros_like(zero)
    picked = [picks[0, j] for j in range(ROUNDS)]

    def clear(b):
        return pltpu.make_async_copy(zero, table_out.at[b], zero_sem.at[b])

    def store(j):
        return pltpu.make_async_copy(acc.at[j], table_out.at[picked[j]], acc_sem.at[j])

    def unused(b):
        return functools.reduce(jnp.logical_and, [p != b for p in picked])

    def first(j):
        return functools.reduce(jnp.logical_and, [picked[i] != picked[j] for i in range(j)], True)

    for b in range(BPD):

        @pl.when(unused(b))
        def _(b=b):
            clear(b).start()

    for j in range(ROUNDS):

        @pl.when(first(j))
        def _(j=j):
            acc[j] = ret[j].astype(jnp.float32)
            for i in range(j + 1, ROUNDS):

                @pl.when(picked[i] == picked[j])
                def _(i=i):
                    acc[j] += ret[i].astype(jnp.float32)

            store(j).start()

    loss_out[...] = loss_in[0:1, 0:1] * (1.0 / (N * MEN))
    for b in range(BPD):

        @pl.when(unused(b))
        def _(b=b):
            clear(b).wait()

    for j in range(ROUNDS):

        @pl.when(first(j))
        def _(j=j):
            store(j).wait()

    dm_copy.wait()


def on_device(mentions, table, picks, gold):
    vmem = pl.BlockSpec(memory_space=pltpu.VMEM)
    anywhere = pl.BlockSpec(memory_space=pl.ANY)
    ret, dm, loss = pl.pallas_call(
        exchange,
        out_shape=(
            pltpu.VMEM((ROUNDS, BLK, D), WIRE),
            pltpu.VMEM((MEN, D), jnp.float32),
            pltpu.VMEM((8, 128), jnp.float32),
        ),
        in_specs=[pl.BlockSpec(memory_space=pltpu.SMEM), anywhere, anywhere, anywhere],
        out_specs=(vmem, vmem, vmem),
        scratch_shapes=[
            *(pltpu.VMEM((BPD, BLK // 4, D), jnp.bfloat16) for _ in range(4)),
            pltpu.VMEM((MEN, D), jnp.bfloat16),
            pltpu.VMEM((8, 128), jnp.int32),
            pltpu.VMEM((STEPS, BLK, D), jnp.bfloat16),
            pltpu.VMEM((STEPS, BLK, D), jnp.bfloat16),
            pltpu.VMEM((STEPS, BLK, MEN), jnp.float32),
            pltpu.VMEM((STEPS, BLK, MEN), jnp.bfloat16),
            pltpu.VMEM((STEPS, BLK, D), WIRE),
            pltpu.VMEM((4, 8, 128), jnp.float32),
            pltpu.VMEM((4, 4, 8, 128), jnp.float32),
            pltpu.SemaphoreType.DMA((6,)),
            pltpu.SemaphoreType.DMA((STEPS,)),
            pltpu.SemaphoreType.DMA((STEPS,)),
            pltpu.SemaphoreType.DMA((1,)),
            pltpu.SemaphoreType.DMA((1,)),
            pltpu.SemaphoreType.DMA((4,)),
            pltpu.SemaphoreType.DMA((4,)),
        ],
        compiler_params=pltpu.CompilerParams(
            collective_id=0, has_side_effects=True, vmem_limit_bytes=56 * 2**20
        ),
        name="exchange",
    )(picks, table.reshape(BPD, BLK, D), mentions, gold.reshape(8, 128))
    d_table, d_mentions, total = pl.pallas_call(
        collect,
        out_shape=(
            jax.ShapeDtypeStruct((BPD, BLK, D), jnp.float32),
            jax.ShapeDtypeStruct((MEN, D), jnp.float32),
            jax.ShapeDtypeStruct((1, 1), jnp.float32),
        ),
        in_specs=[pl.BlockSpec(memory_space=pltpu.SMEM), vmem, vmem, vmem],
        out_specs=(anywhere, anywhere, vmem),
        scratch_shapes=[
            pltpu.VMEM((BLK, D), jnp.float32),
            pltpu.VMEM((ROUNDS, BLK, D), jnp.float32),
            pltpu.SemaphoreType.DMA,
            pltpu.SemaphoreType.DMA((BPD,)),
            pltpu.SemaphoreType.DMA((ROUNDS,)),
        ],
        compiler_params=pltpu.CompilerParams(vmem_limit_bytes=24 * 2**20),
        name="collect",
    )(picks, ret, dm, loss)
    return total.reshape(()), d_mentions, d_table.reshape(BPD * BLK, D)


def solution(mesh):
    return jax.shard_map(
        on_device,
        mesh=mesh,
        in_specs=(P("ent", None), P("ent", None), P("ent", None), P("ent")),
        out_specs=(P(), P("ent", None), P("ent", None)),
        check_vma=False,
    )
```

```python
import functools

import jax
import jax.numpy as jnp
from jax import lax
from jax.experimental import pallas as pl
from jax.experimental.pallas import tpu as pltpu
from jax.sharding import PartitionSpec as P

BLK = 256
ROUNDS = 8
MEN = 1024
D = 768
BPD = 16
N = 128
STRIDE = N // ROUNDS
STEPS = 8
ROWS = BLK // STEPS
AHEAD = 4
WIRE = jnp.bfloat16


def ring_peers(me):
    phases = []
    for weight, length in ((32, 4), (8, 4), (2, 4), (1, 2)):
        at = lax.rem(lax.div(me, weight), length)
        base = me - at * weight
        phases.append((at, [base + lax.rem(at + by, length) * weight for by in range(1, length)]))
    return phases


def exchange(
    picks, table, mentions, gold, ret, dm, loss,
    part_a, part_b, part_c, part_d, part_e, part_f, part_g, part_h, ment_v, gold_v, send, cand, scores, dscore, gsend, lsend, lbuf,
    local_sem, fsend, frecv, bsend, brecv, lsend_sem, lrecv_sem,
):
    me = lax.axis_index("ent")
    parts = (part_a, part_b, part_c, part_d, part_e, part_f, part_g, part_h)
    depth = BLK // len(parts)
    loads = [
        pltpu.make_async_copy(table.at[:, pl.ds(q * depth, depth)], part, local_sem.at[q])
        for q, part in enumerate(parts)
    ]
    load_mentions = pltpu.make_async_copy(mentions, ment_v, local_sem.at[len(parts)])
    load_gold = pltpu.make_async_copy(gold, gold_v, local_sem.at[len(parts) + 1])
    for load in loads:
        load.start()

    ahead = [lax.rem(me + (j * STRIDE + 1), N) for j in range(ROUNDS)]
    behind = [lax.rem(me + (N - j * STRIDE - 1), N) for j in range(ROUNDS)]
    phases = ring_peers(me)
    peers = ahead + behind + [p for _, group in phases for p in group]
    barrier = pltpu.get_barrier_semaphore()
    for peer in peers:
        pl.semaphore_signal(barrier, inc=1, device_id=(peer,), device_id_type=pl.DeviceIdType.MESH)
    load_mentions.start()
    load_gold.start()

    def remote(src, dst, send_sem, recv_sem, device):
        return pltpu.make_async_remote_copy(
            src_ref=src,
            dst_ref=dst,
            send_sem=send_sem,
            recv_sem=recv_sem,
            device_id=(device,),
            device_id_type=pl.DeviceIdType.MESH,
        )

    def wait_for(ref, sem):
        pltpu.make_async_copy(ref, ref, sem).wait()

    def start_forward(c):
        for j in range(ROUNDS):
            remote(
                send.at[c, pl.ds(j * ROWS, ROWS)],
                cand.at[c, pl.ds(j * ROWS, ROWS)],
                fsend.at[c],
                frecv.at[c],
                ahead[j],
            ).start()

    def start_backward(c, which):
        for j in which:
            remote(
                gsend.at[c, pl.ds(j * ROWS, ROWS)],
                ret.at[j, pl.ds(pl.multiple_of(c * ROWS, ROWS), ROWS)],
                bsend.at[0],
                brecv.at[0],
                behind[j],
            ).start()

    for q, part in enumerate(parts):
        loads[q].wait()
        for j in range(ROUNDS):
            block = part[picks[0, j]]
            for h in range(depth // ROWS):
                send[q * (depth // ROWS) + h, j * ROWS : (j + 1) * ROWS] = block[h * ROWS : (h + 1) * ROWS]
        if q == 0:
            pl.semaphore_wait(barrier, len(peers))
        for c in range(q * (depth // ROWS), (q + 1) * (depth // ROWS)):
            if c < AHEAD:
                start_forward(c)

    load_mentions.wait()
    load_gold.wait()
    gold_row = jnp.concatenate([gold_v[r : r + 1, :] for r in range(MEN // 128)], axis=1)
    local = lax.broadcasted_iota(jnp.int32, (BLK, MEN), 0)
    spread = (local // ROWS) * BLK + local % ROWS

    def score_step(c, carry):
        top, total = carry
        wait_for(cand.at[c], frecv.at[c])

        @pl.when(c + AHEAD < STEPS)
        def _():
            wait_for(send.at[c], fsend.at[c])
            start_forward(c + AHEAD)

        scores[c] = lax.dot_general(
            cand[c], ment_v[...], (((1,), (1,)), ((), ())), preferred_element_type=jnp.float32
        )
        here = scores[c]
        newer = jnp.maximum(top, jnp.max(here, axis=0, keepdims=True))
        total = total * jnp.exp(top - newer) + jnp.sum(jnp.exp(here - newer), axis=0, keepdims=True)
        return newer, total

    row = (1, MEN)
    top, total = lax.fori_loop(
        0,
        STEPS,
        score_step,
        (
            jnp.full(row, -jnp.inf, jnp.float32),
            jnp.zeros(row, jnp.float32),
        ),
    )
    lse = top + jnp.log(total)

    def gradient_step(c, target):
        half = BLK // 2
        hit = spread == gold_row - c * ROWS
        for h in range(2):
            rows = slice(h * half, (h + 1) * half)
            d = (jnp.exp(scores[c, rows] - lse) - jnp.where(hit[rows], 1.0, 0.0)).astype(jnp.bfloat16)
            dscore[c, rows] = d
            gsend[c, rows] = jnp.dot(d, ment_v[...], preferred_element_type=jnp.float32).astype(WIRE)
            start_backward(c, range(h * ROUNDS // 2, (h + 1) * ROUNDS // 2))
        return target + jnp.sum(jnp.where(hit, scores[c], 0.0), axis=0, keepdims=True)

    target = lax.fori_loop(0, STEPS, gradient_step, jnp.zeros(row, jnp.float32))

    def start_phase(p, value):
        at, group = phases[p]
        lsend[p] = value
        lbuf[p, at] = value
        for peer in group:
            remote(lsend.at[p], lbuf.at[p, at], lsend_sem.at[p], lrecv_sem.at[p], peer).start()

    def end_phase(p):
        count = len(phases[p][1])
        wait_for(lbuf.at[p, pl.ds(0, count)], lsend_sem.at[p])
        wait_for(lbuf.at[p, pl.ds(0, count)], lrecv_sem.at[p])
        value = lbuf[p, 0]
        for d in range(1, count + 1):
            value = value + lbuf[p, d]
        return value

    start_phase(0, jnp.broadcast_to(jnp.sum(lse - target, axis=1, keepdims=True), (8, 128)))
    tiles = MEN // BLK
    for t in range(tiles):
        columns = pl.ds(t * BLK, BLK)
        dm[columns, :] = lax.dot_general(
            dscore[:, :, columns].reshape(STEPS * BLK, BLK),
            cand[...].reshape(STEPS * BLK, D),
            (((0,), (0,)), ((), ())),
            preferred_element_type=jnp.float32,
        )
        part = end_phase(t)
        if t + 1 < tiles:
            start_phase(t + 1, part)
        else:
            loss[...] = part

    for c in range(STEPS - AHEAD, STEPS):
        wait_for(send.at[c], fsend.at[c])
    wait_for(gsend, bsend.at[0])
    wait_for(ret, brecv.at[0])


def collect(picks, ret, dm_in, loss_in, table_out, dm_out, loss_out, zero, acc, dm_sem, zero_sem, acc_sem):
    dm_copy = pltpu.make_async_copy(dm_in, dm_out, dm_sem)
    dm_copy.start()
    zero[...] = jnp.zeros_like(zero)
    picked = [picks[0, j] for j in range(ROUNDS)]

    def clear(b):
        return pltpu.make_async_copy(zero, table_out.at[b], zero_sem.at[b])

    def store(j):
        return pltpu.make_async_copy(acc.at[j], table_out.at[picked[j]], acc_sem.at[j])

    def unused(b):
        return functools.reduce(jnp.logical_and, [p != b for p in picked])

    def first(j):
        return functools.reduce(jnp.logical_and, [picked[i] != picked[j] for i in range(j)], True)

    for b in range(BPD):

        @pl.when(unused(b))
        def _(b=b):
            clear(b).start()

    for j in range(ROUNDS):

        @pl.when(first(j))
        def _(j=j):
            acc[j] = ret[j].astype(jnp.float32)
            for i in range(j + 1, ROUNDS):

                @pl.when(picked[i] == picked[j])
                def _(i=i):
                    acc[j] += ret[i].astype(jnp.float32)

            store(j).start()

    loss_out[...] = loss_in[0:1, 0:1] * (1.0 / (N * MEN))
    for b in range(BPD):

        @pl.when(unused(b))
        def _(b=b):
            clear(b).wait()

    for j in range(ROUNDS):

        @pl.when(first(j))
        def _(j=j):
            store(j).wait()

    dm_copy.wait()


def on_device(mentions, table, picks, gold):
    vmem = pl.BlockSpec(memory_space=pltpu.VMEM)
    anywhere = pl.BlockSpec(memory_space=pl.ANY)
    ret, dm, loss = pl.pallas_call(
        exchange,
        out_shape=(
            pltpu.VMEM((ROUNDS, BLK, D), WIRE),
            pltpu.VMEM((MEN, D), jnp.float32),
            pltpu.VMEM((8, 128), jnp.float32),
        ),
        in_specs=[pl.BlockSpec(memory_space=pltpu.SMEM), anywhere, anywhere, anywhere],
        out_specs=(vmem, vmem, vmem),
        scratch_shapes=[
            *(pltpu.VMEM((BPD, BLK // 8, D), jnp.bfloat16) for _ in range(8)),
            pltpu.VMEM((MEN, D), jnp.bfloat16),
            pltpu.VMEM((8, 128), jnp.int32),
            pltpu.VMEM((STEPS, BLK, D), jnp.bfloat16),
            pltpu.VMEM((STEPS, BLK, D), jnp.bfloat16),
            pltpu.VMEM((STEPS, BLK, MEN), jnp.float32),
            pltpu.VMEM((STEPS, BLK, MEN), jnp.bfloat16),
            pltpu.VMEM((STEPS, BLK, D), WIRE),
            pltpu.VMEM((4, 8, 128), jnp.float32),
            pltpu.VMEM((4, 4, 8, 128), jnp.float32),
            pltpu.SemaphoreType.DMA((10,)),
            pltpu.SemaphoreType.DMA((STEPS,)),
            pltpu.SemaphoreType.DMA((STEPS,)),
            pltpu.SemaphoreType.DMA((1,)),
            pltpu.SemaphoreType.DMA((1,)),
            pltpu.SemaphoreType.DMA((4,)),
            pltpu.SemaphoreType.DMA((4,)),
        ],
        compiler_params=pltpu.CompilerParams(
            collective_id=0, has_side_effects=True, vmem_limit_bytes=56 * 2**20
        ),
        name="exchange",
    )(picks, table.reshape(BPD, BLK, D), mentions, gold.reshape(8, 128))
    d_table, d_mentions, total = pl.pallas_call(
        collect,
        out_shape=(
            jax.ShapeDtypeStruct((BPD, BLK, D), jnp.float32),
            jax.ShapeDtypeStruct((MEN, D), jnp.float32),
            jax.ShapeDtypeStruct((1, 1), jnp.float32),
        ),
        in_specs=[pl.BlockSpec(memory_space=pltpu.SMEM), vmem, vmem, vmem],
        out_specs=(anywhere, anywhere, vmem),
        scratch_shapes=[
            pltpu.VMEM((BLK, D), jnp.float32),
            pltpu.VMEM((ROUNDS, BLK, D), jnp.float32),
            pltpu.SemaphoreType.DMA,
            pltpu.SemaphoreType.DMA((BPD,)),
            pltpu.SemaphoreType.DMA((ROUNDS,)),
        ],
        compiler_params=pltpu.CompilerParams(vmem_limit_bytes=24 * 2**20),
        name="collect",
    )(picks, ret, dm, loss)
    return total.reshape(()), d_mentions, d_table.reshape(BPD * BLK, D)


def solution(mesh):
    return jax.shard_map(
        on_device,
        mesh=mesh,
        in_specs=(P("ent", None), P("ent", None), P("ent", None), P("ent")),
        out_specs=(P(), P("ent", None), P("ent", None)),
        check_vma=False,
    )
```
